32 devices in a mesh: seq: 4 (over x, core), req: 8 (over z, y).
Axes of the slice: x: 2, y: 2, z: 4, core: 2. Of those that a mesh axis runs over, the one named last changes fastest.
Arguments:
- inputs: bfloat16 [8, 16, 4, 1536], P('req', 'seq'), may hold values from -6 to 6
- parents: int32 [8, 4, 16], P('req'), may hold values from 0 to 15
- block_len: int32 [8, 64], P('req', 'seq'), may hold values from 0 to 128, as said below
- prompt_key_cache: bfloat16 [8, 8192, 512], P('req', 'seq'), may hold values from -230 to 230
- prompt_value_cache: bfloat16 [8, 8192, 512], P('req', 'seq'), may hold values from -6 to 6
- generated_key_cache: bfloat16 [8, 16, 16, 512], P('req', 'seq'), may hold values from -6 to 6
- generated_value_cache: bfloat16 [8, 16, 16, 512], P('req', 'seq'), may hold values from -6 to 6
- gain_attn: float32 [1536], replicated, may hold values from 0.1 to 1.9
- gain_moe: float32 [1536], replicated, may hold values from 0.1 to 1.9
- w_query: bfloat16 [1536, 1536], P(None, 'seq'), may hold values from -0.15625 to 0.15625
- key_projection_weight: bfloat16 [1536, 512], P(None, 'seq'), may hold values from -0.15625 to 0.15625
- value_projection_weight: bfloat16 [1536, 512], P(None, 'seq'), may hold values from -0.15625 to 0.15625
- w_output: bfloat16 [1536, 1536], P('seq'), may hold values from -0.15625 to 0.15625
- w_in: bfloat16 [32, 1536, 1024], P('req'), may hold values from -0.15625 to 0.15625
- w_out: bfloat16 [32, 512, 1536], P('req'), may hold values from -0.25 to 0.25
- routes: int32 [8, 16, 4, 8], P('req', 'seq'), may hold values from 0 to 31, all different within a row; in each aligned block of 16 rows (0 to 15, 16 to 31, ..., all dimensions but the last counted through in order) at most 8 rows name the same one
- gate_weights: float32 [8, 16, 4, 8], P('req', 'seq'), may hold values from 0.05 to 1
Outputs:
- mixed: bfloat16 [8, 16, 4, 1536], P('req', 'seq')
- final_k: bfloat16 [8, 16, 20, 512], P('req', 'seq')
- final_v: bfloat16 [8, 16, 20, 512], P('req', 'seq')
The draws below stay inside these ranges and needn't reach their ends.
Inputs may be any that keep to these rules, and one draw needn't show every extreme that they name: block_len[r, j] is the number of live positions at the start of block j of request r; 0 marks an empty block; the first block of every request is full. `routes`: among the rows of one device (its 4 beams over all 4 steps, in the order beam then step) no expert is named more than 8 times.
All inputs are finite; a program needn't handle non-finite values.
Results may differ from the reference program's by a relative error of at most 0.025.
Values may be sent and summed in bfloat16 or wider, within the bound.
A program may use at most 128 MiB of HBM per device.

```python
import math
import jax
import jax.numpy as jnp
import numpy as np
from jax import lax

MODEL_DIMENSION = 1536
QUERY_HEADS = 24
KEY_VALUE_HEADS = 8
HEAD_SIZE = 64
FFE = 512
TOP = 8
EXPERTS = 32
BEAMS_PER_REQUEST = 16
DECODE_STEPS = 4
BLK = 128
TAIL_TOKENS = 16
REQUEST_COUNT = 8
PROMPT_POSITIONS = 8192
NBLK = 64
BEAM_DEV = 4
MOST = 8


def draw_block_len(key, part):
    key_len = jax.random.fold_in(key, 11)
    key_gap = jax.random.fold_in(key, 12)
    lengths = jax.random.randint(key_len, (REQUEST_COUNT, NBLK), 1, BLK + 1)
    chance = jax.random.randint(key_gap, (REQUEST_COUNT, NBLK), 0, 100)
    column = jnp.arange(NBLK, dtype=jnp.int32)[None, :]
    limit = 75 * column // NBLK
    lengths = jnp.where(chance < limit, 0, lengths)
    lengths = jnp.where(column == 0, BLK, lengths)
    return lengths.astype(jnp.int32)


def draw_prompt_key_cache(key, part):
    feature_width = KEY_VALUE_HEADS * HEAD_SIZE
    base = 2.5 * jnp.clip(jax.random.normal(jax.random.fold_in(key, 21), (REQUEST_COUNT, PROMPT_POSITIONS, feature_width), jnp.float32), -6.0, 6.0)
    return base.astype(jnp.bfloat16)


def set_ends(values, own_key, smallest, largest):
    longest = values.shape.index(max(values.shape))
    spots = []
    for shift in (0, 1):
        where = [jax.random.randint(jax.random.fold_in(own_key, axis), (), 0, length) for axis, length in enumerate(values.shape)]
        where[longest] = (where[longest] + shift) % values.shape[longest]
        spots.append(tuple(where))
    return values.at[spots[0]].set(smallest).at[spots[1]].set(largest)


def level_of(own_key, extent, cuts, least, largest):
    loudness, own = 1.0, jax.random.fold_in(own_key, 6)
    for dim, shards_of in cuts:
        draws = jnp.exp(jax.random.uniform(jax.random.fold_in(own, dim), (shards_of,), jnp.float32, least / len(cuts), largest / len(cuts)))
        loudness = loudness * jnp.repeat(draws, extent[dim] // shards_of).reshape([-1 if axis == dim else 1 for axis in range(len(extent))])
    return loudness


def shared_out(rng, own, number, rows, count, top, most, skew):
    ranking = jax.random.permutation(rng, count)
    crowded, usual = load_shares(count, rows * top, most, skew, True), load_shares(count, rows * top, most, skew, False)
    places = jnp.arange(count)

    def named(sizes, rotation):
        used = int((sizes > 0).sum())
        fixed = max(1, used // 4)
        shifted = fixed + (places - fixed + rotation * (used - fixed)) % max(1, count - fixed)
        return jnp.zeros((count,), jnp.int32).at[ranking[jnp.where(places < fixed, places, shifted)]].set(jnp.asarray(sizes, jnp.int32))

    sizes = jnp.where(number % 4 == 0, named(crowded, number // 4), named(usual, number - number // 4 - 1))
    mixed = jax.random.permutation(jax.random.fold_in(own, 3), count)
    giver, receiver = mixed[0:count // 2 * 2:2], mixed[1:count // 2 * 2:2]
    room = jnp.minimum(sizes[giver] - 1, most - sizes[receiver]) // 2
    room = jnp.where((giver == ranking[0]) | (receiver == ranking[0]) | (sizes[receiver] == 0), 0, jnp.maximum(room, 0))
    shifted = jax.random.randint(jax.random.fold_in(own, 4), (count // 2,), 0, 1 << 20) % (room + 1)
    sizes = sizes.at[giver].add(-shifted).at[receiver].add(shifted)
    members = jnp.searchsorted(jnp.cumsum(sizes), jnp.arange(rows * top), side="right").astype(jnp.int32)
    table = members.reshape(top, rows).T
    table = table[jax.random.permutation(jax.random.fold_in(own, 1), rows)]
    rotation = jax.random.randint(jax.random.fold_in(own, 2), (rows, 1), 0, top)
    return jnp.take_along_axis(table, (jnp.arange(top)[None, :] + rotation) % top, axis=1)


def load_shares(number_of, total, most, skew, full):
    loads = [(1 << 20) // math.isqrt(rank ** skew) + 1 for rank in range(1, number_of + 1)]
    largest = most if full else min(most, max(-(-total // number_of), total * loads[0] // sum(loads)))
    least = 1 if total - largest >= number_of - 1 else 0
    given, rest = [largest] + [least] * (number_of - 1), total - largest - least * (number_of - 1)
    while rest > 0:
        free = [i for i in range(1, number_of) if given[i] < largest] or [i for i in range(1, number_of) if given[i] < most]
        pool, remaining = sum([loads[i] for i in free]), rest
        for i in free:
            extra = min(most - given[i], max(1, remaining * loads[i] // pool), rest)
            given[i] = given[i] + extra
            rest = rest - extra
    return np.array(given)


def scatter_about(stream_key, shape, scale, bound, shards=(), kind=jnp.bfloat16):
    result = jax.random.normal(stream_key, shape, jnp.float32) * scale
    if len(shards) > 0:
        result = level_of(stream_key, shape, shards, -0.22, 0.18) * result
    return jnp.clip(result, min=-bound, max=bound).astype(kind)


def setup_inputs(seed: int = 0) -> dict:
    splits = jax.random.split(jax.random.key(seed), 18)
    inputs = scatter_about(splits[0], (REQUEST_COUNT, BEAMS_PER_REQUEST, DECODE_STEPS, MODEL_DIMENSION), 1.0, 6.0, ((0, 8), (1, 4)))
    parents = set_ends(jax.random.randint(splits[1], (REQUEST_COUNT, DECODE_STEPS, BEAMS_PER_REQUEST), 0, BEAMS_PER_REQUEST), jax.random.fold_in(splits[1], 1), 0, BEAMS_PER_REQUEST - 1).astype(jnp.int32)
    block_len = draw_block_len(jax.random.fold_in(splits[17], 71), 0)
    prompt_key_cache = draw_prompt_key_cache(jax.random.fold_in(splits[17], 71), 0)
    prompt_value_cache = scatter_about(splits[4], (REQUEST_COUNT, PROMPT_POSITIONS, KEY_VALUE_HEADS * HEAD_SIZE), 1.0, 6.0, ((0, 8), (1, 4)))
    generated_key_cache = scatter_about(splits[5], (REQUEST_COUNT, BEAMS_PER_REQUEST, TAIL_TOKENS, KEY_VALUE_HEADS * HEAD_SIZE), 1.0, 6.0, ((0, 8), (1, 4)))
    generated_value_cache = scatter_about(splits[6], (REQUEST_COUNT, BEAMS_PER_REQUEST, TAIL_TOKENS, KEY_VALUE_HEADS * HEAD_SIZE), 1.0, 6.0, ((0, 8), (1, 4)))
    gain_attn = jnp.clip(1.0 + 0.18 * jax.random.normal(splits[7], (MODEL_DIMENSION,), jnp.float32), 0.1, 1.9)
    gain_moe = jnp.clip(1.0 + 0.18 * jax.random.normal(splits[8], (MODEL_DIMENSION,), jnp.float32), 0.1, 1.9)
    w_query = scatter_about(splits[9], (MODEL_DIMENSION, QUERY_HEADS * HEAD_SIZE), MODEL_DIMENSION ** -0.5, 0.15625, ((1, 4),))
    key_projection_weight = scatter_about(splits[10], (MODEL_DIMENSION, KEY_VALUE_HEADS * HEAD_SIZE), MODEL_DIMENSION ** -0.5, 0.15625, ((1, 4),))
    value_projection_weight = scatter_about(splits[11], (MODEL_DIMENSION, KEY_VALUE_HEADS * HEAD_SIZE), MODEL_DIMENSION ** -0.5, 0.15625, ((1, 4),))
    w_output = scatter_about(splits[12], (QUERY_HEADS * HEAD_SIZE, MODEL_DIMENSION), (QUERY_HEADS * HEAD_SIZE) ** -0.5, 0.15625, ((0, 4),))
    w_in = scatter_about(splits[13], (EXPERTS, MODEL_DIMENSION, 2 * FFE), MODEL_DIMENSION ** -0.5, 0.15625, ((0, 8),))
    w_out = scatter_about(splits[14], (EXPERTS, FFE, MODEL_DIMENSION), FFE ** -0.5, 0.25, ((0, 8),))
    routes_keys = jax.random.split(jax.random.fold_in(splits[15], 1), REQUEST_COUNT * BEAMS_PER_REQUEST * DECODE_STEPS // (BEAM_DEV * DECODE_STEPS))
    routes_turns = jax.random.permutation(jax.random.fold_in(splits[15], 3), REQUEST_COUNT * BEAMS_PER_REQUEST * DECODE_STEPS // (BEAM_DEV * DECODE_STEPS))
    routes = jax.vmap(lambda own, number: shared_out(jax.random.fold_in(splits[15], 2), own, number, BEAM_DEV * DECODE_STEPS, EXPERTS, TOP, MOST, 2))(routes_keys, routes_turns).reshape((REQUEST_COUNT, BEAMS_PER_REQUEST, DECODE_STEPS, TOP))
    gate_weights = jnp.clip(jnp.exp(math.log(1.0) - 2.9957323 * jax.random.uniform(splits[16], (REQUEST_COUNT, BEAMS_PER_REQUEST, DECODE_STEPS, TOP), jnp.float32) ** level_of(splits[16], (REQUEST_COUNT, BEAMS_PER_REQUEST, DECODE_STEPS, TOP), ((0, 8), (1, 4)), -0.2, 0.2)), 0.05, 1.0)
    return {"inputs": inputs, "parents": parents, "block_len": block_len, "prompt_key_cache": prompt_key_cache, "prompt_value_cache": prompt_value_cache, "generated_key_cache": generated_key_cache, "generated_value_cache": generated_value_cache, "gain_attn": gain_attn, "gain_moe": gain_moe, "w_query": w_query, "key_projection_weight": key_projection_weight, "value_projection_weight": value_projection_weight, "w_output": w_output, "w_in": w_in, "w_out": w_out, "routes": routes, "gate_weights": gate_weights}


EPSILON = 1e-05
ROPE_BASE = 10000.0
NEGATIVE_FILL = -1e+30
SCORE_SCALE = 0.125

def rms_scale(values, gain_vector):
    values = values.astype(jnp.float32)
    mean_sq = lax.optimization_barrier(jnp.mean(values * values, axis=-1, keepdims=True))
    return values * lax.rsqrt(mean_sq + EPSILON) * gain_vector.astype(jnp.float32)

def apply_rotary(values, token_positions, head_dim):
    lead_shape = values.shape[:-1]
    head_count = values.shape[-1] // head_dim
    shaped = values.reshape(lead_shape + (head_count, head_dim))
    half_dim = head_dim // 2
    frequency = ROPE_BASE ** (-(jnp.arange(half_dim, dtype=jnp.float32) * 2.0 / head_dim))
    angles = token_positions[:, None] * frequency[None, :]
    cosine = jnp.cos(angles)[None, :, None, :]
    sine_part = jnp.sin(angles)[None, :, None, :]
    first_half = shaped[..., :half_dim]
    second = shaped[..., half_dim:]
    turned = jnp.concatenate([first_half * cosine - second * sine_part, second * cosine + first_half * sine_part], axis=-1)
    return turned.reshape(values.shape)

def rounded(values):
    return lax.optimization_barrier(values.astype(jnp.bfloat16)).astype(jnp.float32)

def attend_request(packed, gain_attn, w_query, key_projection_weight, value_projection_weight, w_output):
    inputs, parents, block_len, prompt_key_cache, prompt_value_cache, generated_key_cache, generated_value_cache = packed
    normed = rms_scale(inputs, gain_attn).astype(jnp.bfloat16)
    flattened_rows = normed.reshape(BEAMS_PER_REQUEST * DECODE_STEPS, MODEL_DIMENSION)
    token_positions = jnp.arange(DECODE_STEPS, dtype=jnp.float32) + (PROMPT_POSITIONS + TAIL_TOKENS)
    query_rows = apply_rotary(jnp.dot(flattened_rows, w_query, preferred_element_type=jnp.float32).reshape(BEAMS_PER_REQUEST, DECODE_STEPS, QUERY_HEADS * HEAD_SIZE), token_positions, HEAD_SIZE).astype(jnp.bfloat16)
    updated_keys = apply_rotary(jnp.dot(flattened_rows, key_projection_weight, preferred_element_type=jnp.float32).reshape(BEAMS_PER_REQUEST, DECODE_STEPS, KEY_VALUE_HEADS * HEAD_SIZE), token_positions, HEAD_SIZE).astype(jnp.bfloat16)
    updated_values = jnp.dot(flattened_rows, value_projection_weight, preferred_element_type=jnp.float32).reshape(BEAMS_PER_REQUEST, DECODE_STEPS, KEY_VALUE_HEADS * HEAD_SIZE).astype(jnp.bfloat16)
    prefix_live = (jnp.arange(BLK, dtype=jnp.int32)[None, :] < block_len[:, None]).reshape(PROMPT_POSITIONS)
    prompt_key_rows = prompt_key_cache.reshape(PROMPT_POSITIONS, KEY_VALUE_HEADS, HEAD_SIZE).astype(jnp.float32)
    prompt_value_rows = prompt_value_cache.reshape(PROMPT_POSITIONS, KEY_VALUE_HEADS, HEAD_SIZE).astype(jnp.float32)
    beam_key_cache = generated_key_cache
    beam_value_cache = generated_value_cache
    newest_key = jnp.zeros((BEAMS_PER_REQUEST, DECODE_STEPS, KEY_VALUE_HEADS * HEAD_SIZE), jnp.bfloat16)
    newest_value = jnp.zeros((BEAMS_PER_REQUEST, DECODE_STEPS, KEY_VALUE_HEADS * HEAD_SIZE), jnp.bfloat16)
    outputs = []
    for decode_step_index in range(DECODE_STEPS):
        chosen = parents[decode_step_index]
        beam_key_cache = jnp.take(beam_key_cache, chosen, axis=0)
        beam_value_cache = jnp.take(beam_value_cache, chosen, axis=0)
        newest_key = jnp.take(newest_key, chosen, axis=0).at[:, decode_step_index].set(updated_keys[:, decode_step_index])
        newest_value = jnp.take(newest_value, chosen, axis=0).at[:, decode_step_index].set(updated_values[:, decode_step_index])
        decode_query_step = query_rows[:, decode_step_index].reshape(BEAMS_PER_REQUEST, KEY_VALUE_HEADS, QUERY_HEADS // KEY_VALUE_HEADS, HEAD_SIZE).astype(jnp.float32)
        prefix_scores = jnp.einsum('bgjd,kgd->bgjk', decode_query_step, prompt_key_rows) * SCORE_SCALE
        prefix_mask = prefix_live[None, None, None, :]
        prefix_scores = jnp.where(prefix_mask, prefix_scores, NEGATIVE_FILL)
        beam_key_rows = jnp.concatenate([beam_key_cache, newest_key], axis=1).reshape(BEAMS_PER_REQUEST, TAIL_TOKENS + DECODE_STEPS, KEY_VALUE_HEADS, HEAD_SIZE).astype(jnp.float32)
        beam_value_rows = jnp.concatenate([beam_value_cache, newest_value], axis=1).reshape(BEAMS_PER_REQUEST, TAIL_TOKENS + DECODE_STEPS, KEY_VALUE_HEADS, HEAD_SIZE).astype(jnp.float32)
        own_mask = (jnp.arange(TAIL_TOKENS + DECODE_STEPS, dtype=jnp.int32) <= TAIL_TOKENS + decode_step_index)[None, None, None, :]
        own_scores = jnp.einsum('bgjd,bkgd->bgjk', decode_query_step, beam_key_rows) * SCORE_SCALE
        own_scores = jnp.where(own_mask, own_scores, NEGATIVE_FILL)
        row_max = jnp.maximum(lax.optimization_barrier(jnp.max(prefix_scores, axis=-1)), lax.optimization_barrier(jnp.max(own_scores, axis=-1)))[..., None]
        prefix_weights = jnp.where(prefix_mask, jnp.exp(prefix_scores - row_max), 0.0)
        own_weights = jnp.where(own_mask, jnp.exp(own_scores - row_max), 0.0)
        denominator = lax.optimization_barrier(jnp.sum(prefix_weights, axis=-1)) + lax.optimization_barrier(jnp.sum(own_weights, axis=-1))
        numerator = jnp.einsum('bgjk,kgd->bgjd', rounded(prefix_weights), prompt_value_rows)
        numerator = numerator + jnp.einsum('bgjk,bkgd->bgjd', rounded(own_weights), beam_value_rows)
        attended_heads = (numerator / denominator[..., None]).reshape(BEAMS_PER_REQUEST, QUERY_HEADS * HEAD_SIZE).astype(jnp.bfloat16)
        projected = jnp.dot(attended_heads, w_output, preferred_element_type=jnp.float32)
        outputs.append(inputs[:, decode_step_index].astype(jnp.float32) + projected)
    hidden = jnp.stack(outputs, axis=1)
    return (hidden, jnp.concatenate([beam_key_cache, newest_key], axis=1), jnp.concatenate([beam_value_cache, newest_value], axis=1))

def reference(inputs, parents, block_len, prompt_key_cache, prompt_value_cache, generated_key_cache, generated_value_cache, gain_attn, gain_moe, w_query, key_projection_weight, value_projection_weight, w_output, w_in, w_out, routes, gate_weights):

    def per_request(packed):
        return attend_request(packed, gain_attn, w_query, key_projection_weight, value_projection_weight, w_output)
    hidden, final_k, final_v = lax.map(per_request, (inputs, parents, block_len, prompt_key_cache, prompt_value_cache, generated_key_cache, generated_value_cache))
    row_total = REQUEST_COUNT * BEAMS_PER_REQUEST * DECODE_STEPS
    flat_hidden = hidden.reshape(row_total, MODEL_DIMENSION)
    expert_in = rms_scale(flat_hidden, gain_moe).astype(jnp.bfloat16)
    chosen = routes.reshape(row_total * TOP).astype(jnp.int32)
    pair_gates = gate_weights.reshape(row_total * TOP)
    order = jnp.argsort(chosen, stable=True).astype(jnp.int32)
    expert_ids = jnp.arange(EXPERTS, dtype=jnp.int32)
    counts = lax.optimization_barrier(jnp.sum((chosen[None, :] == expert_ids[:, None]).astype(jnp.int32), axis=1)).astype(jnp.int32)
    starts = (jnp.cumsum(counts) - counts).astype(jnp.int32)
    pair_block = 256
    padded = jnp.concatenate([order, jnp.zeros((pair_block,), jnp.int32)])

    def per_expert(carried, expert_index):
        gate_up = w_in[expert_index]
        down_proj = w_out[expert_index]
        limit = counts[expert_index]
        anchor = starts[expert_index]

        def one_block(block_index, accum):
            offset = (block_index * pair_block).astype(jnp.int32)
            pair_ids = lax.dynamic_slice(padded, ((anchor + offset).astype(jnp.int32),), (pair_block,))
            live = offset + jnp.arange(pair_block, dtype=jnp.int32) < limit
            row_ids = (pair_ids // TOP).astype(jnp.int32)
            picked = jnp.take(expert_in, row_ids, axis=0)
            projected = jnp.dot(picked, gate_up, preferred_element_type=jnp.float32)
            activation = (jax.nn.silu(projected[:, :FFE]) * projected[:, FFE:]).astype(jnp.bfloat16)
            expert_out = rounded(jnp.dot(activation, down_proj, preferred_element_type=jnp.float32))
            scaled = jnp.where(live, jnp.take(pair_gates, pair_ids), 0.0)[:, None] * expert_out
            return accum.at[row_ids].add(scaled)
        trips = ((limit + pair_block - 1) // pair_block).astype(jnp.int32)
        return (lax.fori_loop(jnp.int32(0), trips, one_block, carried), None)
    summed, unused = lax.scan(per_expert, jnp.zeros((row_total, MODEL_DIMENSION), jnp.float32), expert_ids)
    mixed = (flat_hidden + summed).astype(jnp.bfloat16).reshape(REQUEST_COUNT, BEAMS_PER_REQUEST, DECODE_STEPS, MODEL_DIMENSION)
    return (mixed, final_k, final_v)
```

```python
import jax
import jax.numpy as jnp
from jax import lax
from jax.sharding import PartitionSpec as P

QUERY_HEADS = 24
HEAD_SIZE = 64
BLK = 128


EPSILON = 1e-05
ROPE_BASE = 10000.0
NEGATIVE_FILL = -1e30
SCORE_SCALE = 0.125


def rms_scale(values, gain_vector):
    values = values.astype(jnp.float32)
    mean_sq = jnp.mean(values * values, axis=-1, keepdims=True)
    return values * lax.rsqrt(mean_sq + EPSILON) * gain_vector


def apply_rotary(values, token_positions, head_dim):
    lead_shape = values.shape[:-1]
    head_count = values.shape[-1] // head_dim
    shaped = values.reshape(lead_shape + (head_count, head_dim))
    half_dim = head_dim // 2
    frequency = ROPE_BASE ** (-(jnp.arange(half_dim, dtype=jnp.float32) * 2.0 / head_dim))
    angles = token_positions[:, None] * frequency[None, :]
    cosine = jnp.cos(angles)[None, :, None, :]
    sine_part = jnp.sin(angles)[None, :, None, :]
    first_half = shaped[..., :half_dim]
    second = shaped[..., half_dim:]
    turned = jnp.concatenate(
        [first_half * cosine - second * sine_part, second * cosine + first_half * sine_part],
        axis=-1,
    )
    return turned.reshape(values.shape)


def project(row_block, weight):
    flattened_rows = row_block.reshape(-1, row_block.shape[-1])
    result = jnp.dot(flattened_rows, weight, preferred_element_type=jnp.float32)
    return result.reshape(row_block.shape[:-1] + (weight.shape[1],))


def ancestry(parents, beam_count):
    step_count = parents.shape[0]
    rows = beam_count * step_count
    p = parents.T.reshape(rows, 1)
    row = jnp.arange(rows, dtype=jnp.int32)
    t = (row % step_count)[:, None]
    col = row[None, :]
    link = ((t > 0) & (col == p * step_count + t - 1)).astype(jnp.float32)
    eye = (row[:, None] == col).astype(jnp.float32)
    seen = eye + link
    power = link
    for _ in range(step_count - 2):
        power = jnp.dot(power, link)
        seen = seen + power
    first = ((t == 0) & (p == jnp.arange(beam_count, dtype=jnp.int32)[None, :])).astype(jnp.float32)
    return seen, jnp.dot(seen, first)


def attend(
    inputs,
    parents,
    block_len,
    prompt_k,
    prompt_v,
    gen_k,
    gen_v,
    gain_attn,
    w_query,
    w_key,
    w_value,
    w_output,
):
    rows_here, step_count, width = inputs.shape
    n = lax.axis_size("seq")
    me = lax.axis_index("seq")
    beams = rows_here * n
    mine = rows_here * step_count
    rows = beams * step_count
    tail_len, kv_width = gen_k.shape[1:]
    kv_heads = kv_width // HEAD_SIZE
    group = QUERY_HEADS // kv_heads
    hw, kw = w_query.shape[1], w_key.shape[1]
    positions = jnp.arange(step_count, dtype=jnp.float32) + (prompt_k.shape[0] * n + tail_len)
    normed = rms_scale(inputs, gain_attn).astype(jnp.bfloat16)
    normed = lax.all_gather(normed, "seq", axis=0, tiled=True)
    q = apply_rotary(project(normed, w_query), positions, HEAD_SIZE)
    k = apply_rotary(project(normed, w_key), positions, HEAD_SIZE)
    v = project(normed, w_value)
    qkv = jnp.concatenate([q, k, v], axis=-1).astype(jnp.bfloat16).reshape(rows, hw + 2 * kw)
    qkv = lax.all_gather(qkv, "seq", axis=1)
    q = qkv[:, :, :hw].reshape(rows, kv_heads, group, HEAD_SIZE)
    new_k = qkv[:, :, hw : hw + kw].reshape(rows, kv_width)
    new_v = qkv[:, :, hw + kw :].reshape(rows, kv_width)
    seen, owner = ancestry(parents, beams)
    own_mask = jnp.repeat(
        lax.dynamic_slice_in_dim(owner, me * rows_here, rows_here, 1), tail_len, axis=1
    )
    fresh_mask = lax.dynamic_slice_in_dim(seen, me * mine, mine, 1)
    live = (jnp.arange(BLK, dtype=jnp.int32)[None, :] < block_len[:, None]).reshape(1, -1)
    mask = jnp.concatenate(
        [
            jnp.broadcast_to(live, (rows, live.shape[1])),
            own_mask > 0.5,
            fresh_mask > 0.5,
        ],
        axis=1,
    )
    keys = jnp.concatenate(
        [prompt_k, gen_k.reshape(-1, kv_width), lax.dynamic_slice_in_dim(new_k, me * mine, mine)]
    ).reshape(-1, kv_heads, HEAD_SIZE)
    values = jnp.concatenate(
        [prompt_v, gen_v.reshape(-1, kv_width), lax.dynamic_slice_in_dim(new_v, me * mine, mine)]
    ).reshape(-1, kv_heads, HEAD_SIZE)
    scores = jnp.einsum("rgjd,kgd->gjrk", q, keys, preferred_element_type=jnp.float32)
    scores = jnp.where(mask, scores * SCORE_SCALE, NEGATIVE_FILL)
    top = jnp.max(scores, axis=-1)
    weights = jnp.where(mask, jnp.exp(scores - top[..., None]), 0.0)
    total = jnp.sum(weights, axis=-1)
    num = jnp.einsum(
        "gjrk,kgd->gjrd",
        weights.astype(jnp.bfloat16),
        values,
        preferred_element_type=jnp.float32,
    )
    own_heads = QUERY_HEADS // n
    num = lax.all_to_all(
        num.astype(jnp.bfloat16).reshape(n, own_heads, rows, HEAD_SIZE), "seq", 0, 0, tiled=True
    )
    stats = lax.all_to_all(
        jnp.stack([top, total], -1).reshape(n, own_heads, rows, 2), "seq", 0, 0, tiled=True
    )
    top = jnp.max(stats[..., 0], axis=0, keepdims=True)
    scale = jnp.exp(stats[..., 0] - top)
    total = jnp.sum(scale * stats[..., 1], axis=0)
    attended = jnp.sum(scale[..., None] * num.astype(jnp.float32), axis=0) / total[..., None]
    attended = attended.astype(jnp.bfloat16).transpose(1, 0, 2).reshape(rows, hw)
    partial = jnp.dot(attended, w_output, preferred_element_type=jnp.float32)
    partial = lax.all_to_all(
        partial.astype(jnp.bfloat16).reshape(n, mine, width), "seq", 0, 0, tiled=True
    )
    hidden = inputs.reshape(mine, width).astype(jnp.float32) + jnp.sum(
        partial.astype(jnp.float32), axis=0
    )
    last = (jnp.arange(rows_here) + me * rows_here) * step_count + step_count - 1
    own_pick = jnp.argmax(owner[last], axis=1)
    fresh_pick = jnp.argmax(
        seen[last].reshape(rows_here, beams, step_count), axis=1
    ) * step_count + jnp.arange(step_count)
    finals = []
    for gen, new in ((gen_k, new_k), (gen_v, new_v)):
        everyone = lax.all_gather(gen, "seq", axis=0, tiled=True)
        finals.append(
            jnp.concatenate([jnp.take(everyone, own_pick, axis=0), new[fresh_pick]], axis=1)
        )
    return hidden, finals[0], finals[1]


def experts(hidden, gain_moe, w_in, w_out, routes, gates):
    mine, width = hidden.shape
    n = lax.axis_size("req")
    held = w_in.shape[0]
    half = w_out.shape[1]
    normed = rms_scale(hidden, gain_moe).astype(jnp.bfloat16)
    ids = jnp.arange(held * n, dtype=jnp.int32)
    table = jnp.sum(
        jnp.where(routes[:, :, None] == ids[None, None, :], gates[:, :, None], 0.0), axis=1
    )
    sent = table.reshape(mine, n, held).transpose(1, 0, 2)
    table = lax.all_to_all(sent, "req", 0, 0, tiled=True).reshape(n * mine, held)
    rows = lax.all_gather(normed, "req", axis=0, tiled=True)
    summed = jnp.zeros((n * mine, width), jnp.float32)
    for e in range(held):
        projected = jnp.dot(rows, w_in[e], preferred_element_type=jnp.float32)
        act = (jax.nn.silu(projected[:, :half]) * projected[:, half:]).astype(jnp.bfloat16)
        out = jnp.dot(act, w_out[e], preferred_element_type=jnp.float32)
        out = out.astype(jnp.bfloat16).astype(jnp.float32)
        summed = summed + table[:, e : e + 1] * out
    back = lax.all_to_all(
        summed.astype(jnp.bfloat16).reshape(n, mine, width), "req", 0, 0, tiled=True
    )
    return (hidden + jnp.sum(back.astype(jnp.float32), axis=0)).astype(jnp.bfloat16)


def local(
    inputs,
    parents,
    block_len,
    prompt_key_cache,
    prompt_value_cache,
    generated_key_cache,
    generated_value_cache,
    gain_attn,
    gain_moe,
    w_query,
    key_projection_weight,
    value_projection_weight,
    w_output,
    w_in,
    w_out,
    routes,
    gate_weights,
):
    hidden, final_k, final_v = attend(
        inputs[0],
        parents[0],
        block_len[0],
        prompt_key_cache[0],
        prompt_value_cache[0],
        generated_key_cache[0],
        generated_value_cache[0],
        gain_attn,
        w_query,
        key_projection_weight,
        value_projection_weight,
        w_output,
    )
    top = routes.shape[3]
    mixed = experts(
        hidden, gain_moe, w_in, w_out, routes.reshape(-1, top), gate_weights.reshape(-1, top)
    )
    return (mixed.reshape(inputs.shape), final_k[None], final_v[None])


def solution(mesh):
    placed = (
        P("req", "seq", None, None),
        P("req", None, None),
        P("req", "seq"),
        P("req", "seq", None),
        P("req", "seq", None),
        P("req", "seq", None, None),
        P("req", "seq", None, None),
        P(),
        P(),
        P(None, "seq"),
        P(None, "seq"),
        P(None, "seq"),
        P("seq", None),
        P("req", None, None),
        P("req", None, None),
        P("req", "seq", None, None),
        P("req", "seq", None, None),
    )
    return jax.shard_map(
        local,
        mesh=mesh,
        in_specs=placed,
        out_specs=(
            P("req", "seq", None, None),
            P("req", "seq", None, None),
            P("req", "seq", None, None),
        ),
        check_vma=False,
    )
```

```python
from functools import partial

import jax
import jax.numpy as jnp
from jax import lax
from jax.experimental import pallas as pl
from jax.experimental.pallas import tpu as pltpu
from jax.sharding import PartitionSpec as P

QUERY_HEADS = 24
HEAD_SIZE = 64
BLK = 128


EPSILON = 1e-05
ROPE_BASE = 10000.0
NEGATIVE_FILL = -1e30
SCORE_SCALE = 0.125


def rms_scale(values, gain_vector):
    values = values.astype(jnp.float32)
    mean_sq = jnp.mean(values * values, axis=-1, keepdims=True)
    return values * lax.rsqrt(mean_sq + EPSILON) * gain_vector


def apply_rotary(values, token_positions, head_dim):
    lead_shape = values.shape[:-1]
    head_count = values.shape[-1] // head_dim
    shaped = values.reshape(lead_shape + (head_count, head_dim))
    half_dim = head_dim // 2
    frequency = ROPE_BASE ** (-(jnp.arange(half_dim, dtype=jnp.float32) * 2.0 / head_dim))
    angles = token_positions[:, None] * frequency[None, :]
    cosine = jnp.cos(angles)[None, :, None, :]
    sine_part = jnp.sin(angles)[None, :, None, :]
    first_half = shaped[..., :half_dim]
    second = shaped[..., half_dim:]
    turned = jnp.concatenate(
        [first_half * cosine - second * sine_part, second * cosine + first_half * sine_part],
        axis=-1,
    )
    return turned.reshape(values.shape)


def project(row_block, weight):
    flattened_rows = row_block.reshape(-1, row_block.shape[-1])
    result = jnp.dot(flattened_rows, weight, preferred_element_type=jnp.float32)
    return result.reshape(row_block.shape[:-1] + (weight.shape[1],))


def ancestry(parents, beam_count):
    step_count = parents.shape[0]
    rows = beam_count * step_count
    p = parents.T.reshape(rows, 1)
    row = jnp.arange(rows, dtype=jnp.int32)
    t = (row % step_count)[:, None]
    col = row[None, :]
    link = ((t > 0) & (col == p * step_count + t - 1)).astype(jnp.float32)
    eye = (row[:, None] == col).astype(jnp.float32)
    seen = eye + link
    power = link
    for _ in range(step_count - 2):
        power = jnp.dot(power, link)
        seen = seen + power
    first = ((t == 0) & (p == jnp.arange(beam_count, dtype=jnp.int32)[None, :])).astype(jnp.float32)
    return seen, jnp.dot(seen, first)


def attend(
    inputs,
    parents,
    block_len,
    prompt_k,
    prompt_v,
    gen_k,
    gen_v,
    gain_attn,
    w_query,
    w_key,
    w_value,
    w_output,
):
    rows_here, step_count, width = inputs.shape
    n = lax.axis_size("seq")
    me = lax.axis_index("seq")
    beams = rows_here * n
    mine = rows_here * step_count
    rows = beams * step_count
    tail_len, kv_width = gen_k.shape[1:]
    kv_heads = kv_width // HEAD_SIZE
    group = QUERY_HEADS // kv_heads
    hw, kw = w_query.shape[1], w_key.shape[1]
    positions = jnp.arange(step_count, dtype=jnp.float32) + (prompt_k.shape[0] * n + tail_len)
    normed = rms_scale(inputs, gain_attn).astype(jnp.bfloat16)
    normed = lax.all_gather(normed, "seq", axis=0, tiled=True)
    q = apply_rotary(project(normed, w_query), positions, HEAD_SIZE)
    k = apply_rotary(project(normed, w_key), positions, HEAD_SIZE)
    v = project(normed, w_value)
    qkv = jnp.concatenate([q, k, v], axis=-1).astype(jnp.bfloat16).reshape(rows, hw + 2 * kw)
    qkv = lax.all_gather(qkv, "seq", axis=1)
    q = qkv[:, :, :hw].reshape(rows, kv_heads, group, HEAD_SIZE)
    new_k = qkv[:, :, hw : hw + kw].reshape(rows, kv_width)
    new_v = qkv[:, :, hw + kw :].reshape(rows, kv_width)
    seen, owner = ancestry(parents, beams)
    own_mask = jnp.repeat(
        lax.dynamic_slice_in_dim(owner, me * rows_here, rows_here, 1), tail_len, axis=1
    )
    fresh_mask = lax.dynamic_slice_in_dim(seen, me * mine, mine, 1)
    live = (jnp.arange(BLK, dtype=jnp.int32)[None, :] < block_len[:, None]).reshape(1, -1)
    mask = jnp.concatenate(
        [
            jnp.broadcast_to(live, (rows, live.shape[1])),
            own_mask > 0.5,
            fresh_mask > 0.5,
        ],
        axis=1,
    )
    keys = jnp.concatenate(
        [prompt_k, gen_k.reshape(-1, kv_width), lax.dynamic_slice_in_dim(new_k, me * mine, mine)]
    ).reshape(-1, kv_heads, HEAD_SIZE)
    values = jnp.concatenate(
        [prompt_v, gen_v.reshape(-1, kv_width), lax.dynamic_slice_in_dim(new_v, me * mine, mine)]
    ).reshape(-1, kv_heads, HEAD_SIZE)
    scores = jnp.einsum("rgjd,kgd->gjrk", q, keys, preferred_element_type=jnp.float32)
    scores = jnp.where(mask, scores * SCORE_SCALE, NEGATIVE_FILL)
    top = jnp.max(scores, axis=-1)
    weights = jnp.where(mask, jnp.exp(scores - top[..., None]), 0.0)
    total = jnp.sum(weights, axis=-1)
    num = jnp.einsum(
        "gjrk,kgd->gjrd",
        weights.astype(jnp.bfloat16),
        values,
        preferred_element_type=jnp.float32,
    )
    own_heads = QUERY_HEADS // n
    num = lax.all_to_all(
        num.astype(jnp.bfloat16).reshape(n, own_heads, rows, HEAD_SIZE), "seq", 0, 0, tiled=True
    )
    stats = lax.all_to_all(
        jnp.stack([top, total], -1).reshape(n, own_heads, rows, 2), "seq", 0, 0, tiled=True
    )
    top = jnp.max(stats[..., 0], axis=0, keepdims=True)
    scale = jnp.exp(stats[..., 0] - top)
    total = jnp.sum(scale * stats[..., 1], axis=0)
    attended = jnp.sum(scale[..., None] * num.astype(jnp.float32), axis=0) / total[..., None]
    attended = attended.astype(jnp.bfloat16).transpose(1, 0, 2).reshape(rows, hw)
    summed = jnp.dot(attended, w_output, preferred_element_type=jnp.float32)
    summed = lax.all_to_all(
        summed.astype(jnp.bfloat16).reshape(n, mine, width), "seq", 0, 0, tiled=True
    )
    hidden = inputs.reshape(mine, width).astype(jnp.float32) + jnp.sum(
        summed.astype(jnp.float32), axis=0
    )
    last = (jnp.arange(rows_here) + me * rows_here) * step_count + step_count - 1
    own_pick = jnp.argmax(owner[last], axis=1)
    fresh_pick = jnp.argmax(
        seen[last].reshape(rows_here, beams, step_count), axis=1
    ) * step_count + jnp.arange(step_count)
    finals = []
    for gen, new in ((gen_k, new_k), (gen_v, new_v)):
        everyone = lax.all_gather(gen, "seq", axis=0, tiled=True)
        finals.append(
            jnp.concatenate([jnp.take(everyone, own_pick, axis=0), new[fresh_pick]], axis=1)
        )
    return hidden, finals[0], finals[1]


def experts(hidden, gain_moe, w_in, w_out, routes, gates):
    mine, width = hidden.shape
    n = lax.axis_size("req")
    held = w_in.shape[0]
    half = w_out.shape[1]
    normed = rms_scale(hidden, gain_moe).astype(jnp.bfloat16)
    ids = jnp.arange(held * n, dtype=jnp.int32)
    table = jnp.sum(
        jnp.where(routes[:, :, None] == ids[None, None, :], gates[:, :, None], 0.0), axis=1
    )
    sent = table.reshape(mine, n, held).transpose(1, 0, 2)
    table = lax.all_to_all(sent, "req", 0, 0, tiled=True).reshape(n * mine, held)
    rows = lax.all_gather(normed, "req", axis=0, tiled=True)
    summed = jnp.zeros((n * mine, width), jnp.float32)
    for e in range(held):
        projected = jnp.dot(rows, w_in[e], preferred_element_type=jnp.float32)
        act = (jax.nn.silu(projected[:, :half]) * projected[:, half:]).astype(jnp.bfloat16)
        out = jnp.dot(act, w_out[e], preferred_element_type=jnp.float32)
        out = out.astype(jnp.bfloat16).astype(jnp.float32)
        summed = summed + table[:, e : e + 1] * out
    back = lax.all_to_all(
        summed.astype(jnp.bfloat16).reshape(n, mine, width), "req", 0, 0, tiled=True
    )
    return (hidden + jnp.sum(back.astype(jnp.float32), axis=0)).astype(jnp.bfloat16)


def greet(axis, n, me):
    barrier = pltpu.get_barrier_semaphore()
    for d in range(1, n):
        pl.semaphore_signal(
            barrier,
            inc=1,
            device_id={axis: lax.rem(me + d, n)},
            device_id_type=pl.DeviceIdType.MESH,
        )
    pl.semaphore_wait(barrier, n - 1)


def push(source, target, send, recv, axis, peer):
    return pltpu.make_async_remote_copy(
        src_ref=source,
        dst_ref=target,
        send_sem=send,
        recv_sem=recv,
        device_id={axis: peer},
        device_id_type=pl.DeviceIdType.MESH,
    )


def iota(shape, dim):
    return lax.broadcasted_iota(jnp.int32, shape, dim)


def pick(condition):
    return jnp.where(condition, 1.0, 0.0).astype(jnp.bfloat16)


def dot(a, b):
    return jnp.dot(a, b, preferred_element_type=jnp.float32)


def moe_kernel(
    n,
    hidden_ref,
    gain_ref,
    routes_ref,
    gates_ref,
    win_ref,
    wout_ref,
    out_ref,
    rows_all,
    tab_all,
    acc,
    back_send,
    back_recv,
    win,
    wout,
    wsem,
    s_rows,
    r_rows,
    s_tab,
    r_tab,
    s_back,
    r_back,
):
    me = lax.axis_index("req")
    held, width = win.shape[0], win.shape[1]
    half = wout.shape[1]
    mine = hidden_ref.shape[0]
    for e in range(held):
        pltpu.make_async_copy(win_ref.at[e], win.at[e], wsem.at[0, e]).start()
        pltpu.make_async_copy(wout_ref.at[e], wout.at[e], wsem.at[1, e]).start()
    greet("req", n, me)
    rows_all[me] = rms_scale(hidden_ref[...], gain_ref[...]).astype(jnp.bfloat16)
    table = jnp.zeros((mine, 128), jnp.float32)
    for j in range(routes_ref.shape[1]):
        table = table + jnp.where(
            iota((mine, 128), 1) == routes_ref[:, j : j + 1], gates_ref[:, j : j + 1], 0.0
        )
    tab_all[me] = table
    copies = []
    for d in range(1, n):
        peer = lax.rem(me + d, n)
        i = d - 1
        copies.append(push(rows_all.at[me], rows_all.at[me], s_rows.at[i], r_rows.at[i], "req", peer))
        copies.append(push(tab_all.at[me], tab_all.at[me], s_tab.at[i], r_tab.at[i], "req", peer))
    for c in copies:
        c.start()
    for c in copies:
        c.wait()
    acc[...] = jnp.zeros_like(acc)

    def one(e, carry):
        pltpu.make_async_copy(win_ref.at[e], win.at[e], wsem.at[0, e]).wait()
        pltpu.make_async_copy(wout_ref.at[e], wout.at[e], wsem.at[1, e]).wait()
        x = rows_all[...].reshape(n * mine, width)
        p = dot(x, win[e])
        g = p[:, :half]
        act = (g / (1.0 + jnp.exp(-g)) * p[:, half:]).astype(jnp.bfloat16)
        o = dot(act, wout[e]).astype(jnp.bfloat16).astype(jnp.float32)
        tab = tab_all[...].reshape(n * mine, 128)
        w = jnp.sum(
            jnp.where(iota((n * mine, 128), 1) == me * held + e, tab, 0.0), axis=1, keepdims=True
        )
        acc[...] += w * o
        return carry

    lax.fori_loop(0, held, one, 0)
    back_send[...] = acc[...].astype(jnp.bfloat16).reshape(n, mine, width)
    copies = []
    for d in range(1, n):
        peer = lax.rem(me + d, n)
        i = d - 1
        copies.append(
            push(back_send.at[peer], back_recv.at[me], s_back.at[i], r_back.at[i], "req", peer)
        )
    for c in copies:
        c.start()
    back_recv[me] = back_send[me]
    for c in copies:
        c.wait()
    out_ref[...] = (
        hidden_ref[...] + jnp.sum(back_recv[...].astype(jnp.float32), axis=0)
    ).astype(jnp.bfloat16)


def experts_kernel(hidden, gain_moe, w_in, w_out, routes, gates):
    n = lax.axis_size("req")
    mine, width = hidden.shape
    vmem = pl.BlockSpec(memory_space=pltpu.VMEM)
    hbm = pl.BlockSpec(memory_space=pl.ANY)
    dma = pltpu.SemaphoreType.DMA
    return pl.pallas_call(
        partial(moe_kernel, n),
        out_shape=jax.ShapeDtypeStruct((mine, width), jnp.bfloat16),
        in_specs=[vmem] * 4 + [hbm] * 2,
        out_specs=vmem,
        scratch_shapes=[
            pltpu.VMEM((n, mine, width), jnp.bfloat16),
            pltpu.VMEM((n, mine, 128), jnp.float32),
            pltpu.VMEM((n * mine, width), jnp.float32),
            pltpu.VMEM((n, mine, width), jnp.bfloat16),
            pltpu.VMEM((n, mine, width), jnp.bfloat16),
            pltpu.VMEM(w_in.shape, jnp.bfloat16),
            pltpu.VMEM(w_out.shape, jnp.bfloat16),
            dma((2, w_in.shape[0])),
        ]
        + [dma((n - 1,))] * 6,
        compiler_params=pltpu.CompilerParams(
            collective_id=1, has_side_effects=True, vmem_limit_bytes=48 << 20
        ),
        name="moe",
    )(hidden, gain_moe[None], routes, gates, w_in, w_out)


def attend_body(
    n,
    steps,
    tail,
    x_ref,
    parents_ref,
    bias_ref,
    cos_ref,
    sin_ref,
    gain_ref,
    gk_ref,
    gv_ref,
    pk_ref,
    pv_ref,
    wq_ref,
    wk_ref,
    wv_ref,
    wo_ref,
    hidden_ref,
    ownk_ref,
    ownv_ref,
    freshk_ref,
    freshv_ref,
    xall,
    gkall,
    gvall,
    qall,
    num_send,
    num_recv,
    st_send,
    st_recv,
    part_send,
    part_recv,
    pk,
    pv,
    wq,
    wk,
    wv,
    wo,
    lsem,
    sx,
    rx,
    sgk,
    rgk,
    sgv,
    rgv,
    sq,
    rq,
    sn,
    rn,
    ss,
    rs,
    sp,
    rp,
):
    me = lax.axis_index("seq")
    mine, width = x_ref.shape
    rows = mine * n
    here = mine // steps
    beams = here * n
    own = here * tail
    hw, kw = wq.shape[1], wk.shape[1]
    heads = hw // HEAD_SIZE
    trio = heads // 2
    pairs = [(wq_ref, wq), (wk_ref, wk), (wv_ref, wv), (pk_ref, pk), (pv_ref, pv)]
    for j in range(trio):
        for side in range(2):
            at = (j + side * trio) * HEAD_SIZE
            to = side * HEAD_SIZE
            pairs.append((wo_ref.at[pl.ds(at, HEAD_SIZE)], wo.at[j, pl.ds(to, HEAD_SIZE)]))
    local_copies = [pltpu.make_async_copy(a, b, lsem.at[i]) for i, (a, b) in enumerate(pairs)]
    for c in local_copies:
        c.start()
    greet("seq", n, me)
    xall[me] = rms_scale(x_ref[...], gain_ref[...]).astype(jnp.bfloat16)
    gkall[me] = gk_ref[...]
    gvall[me] = gv_ref[...]

    def spread(buffer, send, recv):
        made = [
            push(buffer.at[me], buffer.at[me], send.at[d - 1], recv.at[d - 1], "seq", lax.rem(me + d, n))
            for d in range(1, n)
        ]
        for c in made:
            c.start()
        return made

    x_copies = spread(xall, sx, rx)
    cache_copies = spread(gkall, sgk, rgk) + spread(gvall, sgv, rgv)
    for c in local_copies[:3] + x_copies:
        c.wait()
    x = xall[...].reshape(rows, width)
    lane = iota((rows, 128), 1)
    left = lane < HEAD_SIZE
    early = lax.rem(lane, HEAD_SIZE) < HEAD_SIZE // 2

    def rope(values):
        turned = jnp.where(
            early, -pltpu.roll(values, 128 - HEAD_SIZE // 2, 1), pltpu.roll(values, HEAD_SIZE // 2, 1)
        )
        return values * cos_ref[...] + turned * sin_ref[...]

    q = dot(x, wq[...])
    c = [rope(q[:, 128 * i : 128 * i + 128]) for i in range(hw // 128)]
    packed = [
        jnp.where(left, c[0], c[1]),
        jnp.where(left, pltpu.roll(c[0], HEAD_SIZE, 1), pltpu.roll(c[2], HEAD_SIZE, 1)),
        jnp.where(left, c[1], c[2]),
        rope(dot(x, wk[...])),
        dot(x, wv[...]),
    ]
    for i, value in enumerate(packed):
        qall[me, :, 128 * i : 128 * i + 128] = value.astype(jnp.bfloat16)
    q_copies = spread(qall, sq, rq)

    spots = iota((rows, rows), 0)
    cols = iota((rows, rows), 1)
    by_step = pick(lax.rem(iota((rows, steps), 0), steps) == iota((rows, steps), 1))
    table = dot(by_step, parents_ref[...].astype(jnp.float32).astype(jnp.bfloat16))
    beam_of = lax.div(iota((rows, beams), 0), steps)
    parent = jnp.sum(
        jnp.where(beam_of == iota((rows, beams), 1), table, 0.0), axis=1, keepdims=True
    ).astype(jnp.int32)
    t = lax.rem(spots, steps)
    link = pick((t > 0) & (cols == parent * steps + t - 1))
    seen = pick(spots == cols) + link
    power = link
    for _ in range(steps - 2):
        power = dot(power, link).astype(jnp.bfloat16)
        seen = seen + power
    first = pick(
        (lax.rem(iota((rows, beams), 0), steps) == 0) & (parent == iota((rows, beams), 1))
    )
    owner = dot(seen, first).astype(jnp.bfloat16)
    total_tail = own + rows
    key = iota((beams, total_tail), 1)
    to_own = pick((key < own) & (iota((beams, total_tail), 0) == me * here + lax.div(key, tail)))
    key = iota((rows, total_tail), 1)
    to_new = pick(
        (key >= own) & (key < own + mine) & (iota((rows, total_tail), 0) == me * mine + key - own)
    )
    allowed = dot(owner, to_own) + dot(seen, to_new)
    tail_bias = jnp.where(allowed > 0.5, 0.0, NEGATIVE_FILL)
    tail_bias = jnp.concatenate([tail_bias] * heads, axis=0)
    mover = pick((spots < mine) & (cols == me * mine + spots))
    for c in local_copies[3:] + q_copies:
        c.wait()

    def block(i, carry):
        h = lax.rem(me + 1 + i, n)
        at = pl.ds(pl.multiple_of(h * 128, 128), 128)
        q = qall[h, :, :hw]
        tiles = [q[:, 128 * j : 128 * j + 128] * jnp.bfloat16(SCORE_SCALE) for j in range(trio)]
        zero = jnp.zeros((rows, 128), jnp.bfloat16)
        q = jnp.concatenate(
            [jnp.where(left, a, zero) for a in tiles] + [jnp.where(left, zero, a) for a in tiles],
            axis=0,
        )
        new = dot(mover, qall[h, :, hw:]).astype(jnp.bfloat16)
        tail_k = jnp.concatenate([gk_ref[:, at], new[:, :kw]], axis=0)
        tail_v = jnp.concatenate([gv_ref[:, at], new[:, kw:]], axis=0)
        over = (((1,), (1,)), ((), ()))
        s1 = lax.dot_general(q, pk[:, at], over, preferred_element_type=jnp.float32) + bias_ref[...]
        s2 = lax.dot_general(q, tail_k, over, preferred_element_type=jnp.float32) + tail_bias
        top = jnp.maximum(
            jnp.max(s1, axis=1, keepdims=True), jnp.max(s2, axis=1, keepdims=True)
        )
        e1 = jnp.exp(s1 - top)
        e2 = jnp.exp(s2 - top)
        total = jnp.sum(e1, axis=1, keepdims=True) + jnp.sum(e2, axis=1, keepdims=True)
        o = dot(e1.astype(jnp.bfloat16), pv[:, at]) + dot(e2.astype(jnp.bfloat16), tail_v)
        cut = trio * rows
        wide = iota((cut, 128), 1) < HEAD_SIZE
        num_send[h] = jnp.where(wide, o[:cut], o[cut:]).astype(jnp.bfloat16)
        place = iota((heads * rows, 128), 1)
        stats = jnp.where(place == 0, top, jnp.where(place == 1, total, 0.0))
        st_send[h] = stats.T[:8]

        @pl.when(i < n - 1)
        def _():
            push(num_send.at[h], num_recv.at[me], sn.at[i], rn.at[i], "seq", h).start()
            push(st_send.at[h], st_recv.at[me], ss.at[i], rs.at[i], "seq", h).start()

        return carry

    lax.fori_loop(0, n, block, 0)
    num_recv[me] = num_send[me]
    st_recv[me] = st_send[me]
    for i in range(n - 1):
        h = lax.rem(me + 1 + i, n)
        push(num_send.at[h], num_recv.at[me], sn.at[i], rn.at[i], "seq", h).wait()
        push(st_send.at[h], st_recv.at[me], ss.at[i], rs.at[i], "seq", h).wait()
    stats = [st_recv[i] for i in range(n)]
    top = stats[0][0:1]
    for a in stats[1:]:
        top = jnp.maximum(top, a[0:1])
    scales = [jnp.exp(a[0:1] - top) for a in stats]
    total = scales[0] * stats[0][1:2]
    for a, b in zip(scales[1:], stats[1:]):
        total = total + a * b[1:2]
    cut = trio * rows
    wide = iota((cut, 128), 1) < HEAD_SIZE
    mix = jnp.zeros((cut, 128), jnp.float32)
    for i in range(n):
        flat = jnp.broadcast_to(scales[i] / total, (128, heads * rows)).T
        mix = mix + jnp.where(wide, flat[:cut], flat[cut:]) * num_recv[i].astype(jnp.float32)
    mix = mix.astype(jnp.bfloat16)
    result = dot(mix[:rows], wo[0])
    for j in range(1, trio):
        result = result + dot(mix[j * rows : (j + 1) * rows], wo[j])
    part_send[...] = result.astype(jnp.bfloat16).reshape(n, mine, width)
    parts = []
    for d in range(1, n):
        peer = lax.rem(me + d, n)
        parts.append(
            push(part_send.at[peer], part_recv.at[me], sp.at[d - 1], rp.at[d - 1], "seq", peer)
        )
    for c in parts:
        c.start()
    part_recv[me] = part_send[me]

    for c in cache_copies:
        c.wait()
    last_own = pick(
        iota((own, rows), 1)
        == (me * here + lax.div(iota((own, rows), 0), tail)) * steps + steps - 1
    )
    owner_last = dot(last_own, owner).astype(jnp.bfloat16)
    cells = beams * tail
    expand = pick(lax.div(iota((beams, cells), 1), tail) == iota((beams, cells), 0))
    same = lax.rem(iota((own, cells), 0), tail) == lax.rem(iota((own, cells), 1), tail)
    choose = pick(same & (dot(owner_last, expand) > 0.5))
    ownk_ref[...] = dot(choose, gkall[...].reshape(cells, gk_ref.shape[1])).astype(jnp.bfloat16)
    ownv_ref[...] = dot(choose, gvall[...].reshape(cells, gv_ref.shape[1])).astype(jnp.bfloat16)
    last_new = pick(
        iota((mine, rows), 1)
        == (me * here + lax.div(iota((mine, rows), 0), steps)) * steps + steps - 1
    )
    same = lax.rem(iota((mine, rows), 0), steps) == lax.rem(iota((mine, rows), 1), steps)
    choose = pick(same & (dot(last_new, seen) > 0.5))
    for i in range(n):
        new = dot(choose, qall[i, :, hw:]).astype(jnp.bfloat16)
        freshk_ref[:, kw * i : kw * i + kw] = new[:, :kw]
        freshv_ref[:, kw * i : kw * i + kw] = new[:, kw:]
    for c in parts:
        c.wait()
    hidden_ref[...] = x_ref[...].astype(jnp.float32) + jnp.sum(
        part_recv[...].astype(jnp.float32), axis=0
    )


def attend_kernel(
    inputs,
    parents,
    block_len,
    prompt_k,
    prompt_v,
    gen_k,
    gen_v,
    gain_attn,
    w_query,
    w_key,
    w_value,
    w_output,
):
    here, steps, width = inputs.shape
    n = lax.axis_size("seq")
    mine = here * steps
    rows = mine * n
    tail, kv_width = gen_k.shape[1:]
    hw, kw = w_query.shape[1], w_key.shape[1]
    heads = hw // HEAD_SIZE
    half = HEAD_SIZE // 2
    positions = jnp.arange(steps, dtype=jnp.float32) + (prompt_k.shape[0] * n + tail)
    frequency = ROPE_BASE ** (-(jnp.arange(half, dtype=jnp.float32) * 2.0 / HEAD_SIZE))
    angles = jnp.tile(positions[:, None] * frequency[None, :], (here * n, 128 // half))
    live = (jnp.arange(BLK, dtype=jnp.int32)[None, :] < block_len[:, None]).reshape(1, -1)
    bias = jnp.where(live, 0.0, NEGATIVE_FILL).astype(jnp.float32)
    vmem = pl.BlockSpec(memory_space=pltpu.VMEM)
    hbm = pl.BlockSpec(memory_space=pl.ANY)
    dma = pltpu.SemaphoreType.DMA
    bf, f32 = jnp.bfloat16, jnp.float32
    own = here * tail
    hidden, own_k, own_v, fresh_k, fresh_v = pl.pallas_call(
        partial(attend_body, n, steps, tail),
        out_shape=[
            jax.ShapeDtypeStruct((mine, width), f32),
            jax.ShapeDtypeStruct((own, kv_width), bf),
            jax.ShapeDtypeStruct((own, kv_width), bf),
            jax.ShapeDtypeStruct((mine, kv_width), bf),
            jax.ShapeDtypeStruct((mine, kv_width), bf),
        ],
        in_specs=[vmem] * 8 + [hbm] * 6,
        out_specs=[vmem] * 5,
        scratch_shapes=[
            pltpu.VMEM((n, mine, width), bf),
            pltpu.VMEM((n, own, kv_width), bf),
            pltpu.VMEM((n, own, kv_width), bf),
            pltpu.VMEM((n, rows, hw + 2 * kw), bf),
            pltpu.VMEM((n, heads // 2 * rows, 128), bf),
            pltpu.VMEM((n, heads // 2 * rows, 128), bf),
            pltpu.VMEM((n, 8, heads * rows), f32),
            pltpu.VMEM((n, 8, heads * rows), f32),
            pltpu.VMEM((n, mine, width), bf),
            pltpu.VMEM((n, mine, width), bf),
            pltpu.VMEM(prompt_k.shape, bf),
            pltpu.VMEM(prompt_v.shape, bf),
            pltpu.VMEM(w_query.shape, bf),
            pltpu.VMEM(w_key.shape, bf),
            pltpu.VMEM(w_value.shape, bf),
            pltpu.VMEM((heads // 2, 128, width), bf),
            dma((5 + heads,)),
        ]
        + [dma((n - 1,))] * 14,
        compiler_params=pltpu.CompilerParams(
            collective_id=0, has_side_effects=True, vmem_limit_bytes=48 << 20
        ),
        name="attend",
    )(
        inputs.reshape(mine, width),
        parents,
        bias,
        jnp.cos(angles),
        jnp.sin(angles),
        gain_attn[None],
        gen_k.reshape(own, kv_width),
        gen_v.reshape(own, kv_width),
        prompt_k,
        prompt_v,
        w_query,
        w_key,
        w_value,
        w_output,
    )
    finals = [
        jnp.concatenate(
            [a.reshape(here, tail, kv_width), b.reshape(here, steps, kv_width)], axis=1
        )
        for a, b in ((own_k, fresh_k), (own_v, fresh_v))
    ]
    return hidden, finals[0], finals[1]


def local(
    inputs,
    parents,
    block_len,
    prompt_key_cache,
    prompt_value_cache,
    generated_key_cache,
    generated_value_cache,
    gain_attn,
    gain_moe,
    w_query,
    key_projection_weight,
    value_projection_weight,
    w_output,
    w_in,
    w_out,
    routes,
    gate_weights,
):
    in_tiles = (
        w_query.shape[1] == 384
        and key_projection_weight.shape[1] == 128
        and inputs.shape[1] * inputs.shape[2] % 16 == 0
    )
    hidden, final_k, final_v = (attend_kernel if in_tiles else attend)(
        inputs[0],
        parents[0],
        block_len[0],
        prompt_key_cache[0],
        prompt_value_cache[0],
        generated_key_cache[0],
        generated_value_cache[0],
        gain_attn,
        w_query,
        key_projection_weight,
        value_projection_weight,
        w_output,
    )
    top = routes.shape[3]
    mixed = (experts_kernel if in_tiles else experts)(
        hidden, gain_moe, w_in, w_out, routes.reshape(-1, top), gate_weights.reshape(-1, top)
    )
    return (mixed.reshape(inputs.shape), final_k[None], final_v[None])


def solution(mesh):
    placed = (
        P("req", "seq", None, None),
        P("req", None, None),
        P("req", "seq"),
        P("req", "seq", None),
        P("req", "seq", None),
        P("req", "seq", None, None),
        P("req", "seq", None, None),
        P(),
        P(),
        P(None, "seq"),
        P(None, "seq"),
        P(None, "seq"),
        P("seq", None),
        P("req", None, None),
        P("req", None, None),
        P("req", "seq", None, None),
        P("req", "seq", None, None),
    )
    return jax.shard_map(
        local,
        mesh=mesh,
        in_specs=placed,
        out_specs=(
            P("req", "seq", None, None),
            P("req", "seq", None, None),
            P("req", "seq", None, None),
        ),
        check_vma=False,
    )
```
